32 devices in a mesh: dp: 2 (over y), row: 2 (over core), col: 8 (over z, x).
Axes of the slice: x: 2, y: 2, z: 4, core: 2. Of those that a mesh axis runs over, the one named last changes fastest.
Arguments:
- gate_pre: bfloat16 [512, 28672], P(('dp', 'row'), 'col'), may hold values from -6 to 6
- up_pre: bfloat16 [512, 28672], P(('dp', 'row'), 'col'), may hold values from -6 to 6
- grad_out: bfloat16 [512, 16384], P('col', ('dp', 'row')), may hold values from -6 to 6
- down_weight: bfloat16 [28672, 16384], P('col', ('dp', 'row')), may hold values from -0.046875 to 0.046875
- basis: bfloat16 [512, 28672], P(('dp', 'row'), 'col'), may hold values from -0.046875 to 0.046875
- first_moment_in: float32 [512, 16384], P('col', ('dp', 'row')), may hold values from -6 to 6
- second_moment_in: float32 [512, 16384], P('col', ('dp', 'row')), may hold values from 0.1 to 10
Outputs:
- grad_gate: bfloat16 [512, 28672], P(('dp', 'row'), 'col')
- grad_up: bfloat16 [512, 28672], P(('dp', 'row'), 'col')
- scaled_grad: bfloat16 [28672, 16384], P('col', ('dp', 'row'))
- first_moment: float32 [512, 16384], P('col', ('dp', 'row'))
- second_moment: float32 [512, 16384], P('col', ('dp', 'row'))
The draws below stay inside these ranges and needn't reach their ends.
All inputs are finite; a program needn't handle non-finite values.
Results may differ from the reference program's by a relative error of at most 0.024.
Values may be sent and summed in bfloat16 or wider, within the bound.
A program may use at most 128 MiB of HBM per device.

```python
import math
import jax
import jax.numpy as jnp
from jax import lax

D = 16384
FF = 28672
RANK = 512
TOKENS = 512
N_DP = 2
N_ROW = 2


def raised(drawn, stream_key, source, target, blocks, factor):
    def block_of(position):
        return (jnp.arange(drawn.shape[position]) // (drawn.shape[position] // blocks)).reshape((-1,) + (1,) * (drawn.ndim - 1 - position))

    first = jax.random.permutation(stream_key, blocks)[block_of(target)]
    other_side = (block_of(target) + blocks // 2) % blocks
    return jnp.where((block_of(source) == first) | (block_of(source) == other_side), factor * drawn, drawn)


def steps_of(stream_key, extent, split, smallest, largest):
    factor_of, own = 1.0, jax.random.fold_in(stream_key, 6)
    for dim, blocks in split:
        steps = jnp.exp(jax.random.uniform(jax.random.fold_in(own, dim), (blocks,), jnp.float32, smallest / len(split), largest / len(split)))
        factor_of = factor_of * jnp.repeat(steps, extent[dim] // blocks).reshape([-1 if axis == dim else 1 for axis in range(len(extent))])
    return factor_of


def noise(rng, dims, scale, bound, cuts=(), held_as=jnp.bfloat16):
    array = scale * jax.random.normal(rng, dims, jnp.float32)
    if cuts:
        array = array * steps_of(rng, dims, cuts, -0.22, 0.18)
    return jnp.clip(array, -bound, bound).astype(held_as)


def gaussian_with(key, extent, width, limit, pieces, heavy, kind=jnp.bfloat16):
    values = width * jax.random.normal(key, extent, jnp.float32)
    if pieces:
        values = values * steps_of(key, extent, pieces, -0.22, 0.18)
    return jnp.clip(raised(values, jax.random.fold_in(key, 3), *heavy), -limit, limit).astype(kind)


def setup_inputs(seed: int = 0) -> dict:
    splits = jax.random.split(jax.random.key(seed), 8)
    return {
        "gate_pre": noise(splits[0], (TOKENS, FF), 1.0, 6.0, ((0, 4), (1, 8))),
        "up_pre": noise(splits[1], (TOKENS, FF), 1.0, 6.0, ((0, 4), (1, 8))),
        "grad_out": gaussian_with(splits[2], (TOKENS, D), 1.0, 6.0, ((0, 8), (1, 4)), (1, 0, 8, 2.0)),
        "down_weight": noise(splits[3], (FF, D), D ** -0.5, 0.046875, ((0, 8), (1, 4))),
        "basis": gaussian_with(splits[4], (RANK, FF), FF ** -0.5, 0.046875, ((0, 4), (1, 8)), (1, 0, 8, 2.0)),
        "first_moment_in": noise(splits[5], (RANK, D), 1.0, 6.0, ((0, 8), (1, 4)), jnp.float32),
        "second_moment_in": jnp.clip(jnp.exp(math.log(10.0) - 4.6051702 * jax.random.uniform(splits[6], (RANK, D), jnp.float32) ** steps_of(splits[6], (RANK, D), ((0, 8), (1, 4)), -0.2, 0.2)), 0.1, 10.0),
    }


first_fix = 1.0 - math.exp(1000.0 * math.log(0.9))
second_fix = 1.0 - math.exp(1000.0 * math.log(0.999))

def reference(gate_pre, up_pre, grad_out, down_weight, basis, first_moment_in, second_moment_in):
    gate_f = gate_pre.astype(jnp.float32)
    up_f = up_pre.astype(jnp.float32)
    sigma = jax.nn.sigmoid(gate_f)
    act_value = gate_f * sigma
    hidden = (act_value * up_f).astype(jnp.bfloat16)
    block_count = N_DP * N_ROW
    block_width = D // block_count
    out_blocks = grad_out.reshape(TOKENS, block_count, block_width)
    weight_blocks = down_weight.reshape(FF, block_count, block_width)

    def add_block(block_idx, running):
        out_part = lax.dynamic_index_in_dim(out_blocks, block_idx, 1, keepdims=False)
        weight_part = lax.dynamic_index_in_dim(weight_blocks, block_idx, 1, keepdims=False)
        partial_term = lax.dot_general(out_part, weight_part, (((1,), (1,)), ((), ())), preferred_element_type=jnp.float32)
        rounded = lax.optimization_barrier(partial_term.astype(jnp.bfloat16))
        return running + rounded.astype(jnp.float32)
    summed = lax.fori_loop(0, block_count, add_block, jnp.zeros((TOKENS, FF), jnp.float32))
    grad_hidden = lax.optimization_barrier(summed.astype(jnp.bfloat16)).astype(jnp.float32)
    grad_up = (grad_hidden * act_value).astype(jnp.bfloat16)
    grad_gate = (grad_hidden * up_f * sigma * (1.0 + gate_f * (1.0 - sigma))).astype(jnp.bfloat16)
    grad_weight = lax.dot_general(hidden, grad_out, (((0,), (0,)), ((), ())), preferred_element_type=jnp.float32).astype(jnp.bfloat16)
    token_proj = lax.dot_general(basis, hidden, (((1,), (1,)), ((), ())), preferred_element_type=jnp.float32)
    projected = jnp.dot(token_proj, grad_out.astype(jnp.float32), precision=lax.Precision.HIGHEST)
    first_moment = 0.9 * first_moment_in + 0.1 * projected
    second_moment = 0.999 * second_moment_in + 0.001 * projected * projected
    adapted = first_moment / first_fix / (jnp.sqrt(second_moment / second_fix) + 1e-06)
    column_scale = jnp.sqrt(lax.optimization_barrier(jnp.sum(adapted * adapted, axis=0))) / (jnp.sqrt(lax.optimization_barrier(jnp.sum(projected * projected, axis=0))) + 1e-06)
    scaled_grad = (grad_weight.astype(jnp.float32) * column_scale[None, :]).astype(jnp.bfloat16)
    return (grad_gate, grad_up, scaled_grad, first_moment, second_moment)
```

```python
import functools
import math

import jax
import jax.numpy as jnp
from jax import lax
from jax.experimental import pallas as pl
from jax.experimental.pallas import tpu as pltpu
from jax.sharding import PartitionSpec as P

first_fix = 1.0 - math.exp(1000.0 * math.log(0.9))
second_fix = 1.0 - math.exp(1000.0 * math.log(0.999))

CONTRACT_LAST = (((1,), (1,)), ((), ()))


def width_of(extent, most):
    best = 128
    for width in range(128, most + 1, 128):
        if extent % width == 0:
            best = width
    return best


def remote(src, dst, send_sem, recv_sem, device):
    return pltpu.make_async_remote_copy(
        src_ref=src,
        dst_ref=dst,
        send_sem=send_sem,
        recv_sem=recv_sem,
        device_id=device,
        device_id_type=pl.DeviceIdType.MESH,
    )


def kernel(
    n_dp, n_row, n_col, tile, wide,
    gate, up, cot_in, weight, basis_in, first_in, second_in,
    grad_gate, grad_up, first_out, second_out, scale_out, cot_out, hid_out,
    cot, hid, basis, wt, part, recv1, half, recv2, tok_send, tok_recv, tok_all, sums,
    local_sem, w_sem, ring_s, ring_r, bas_s, bas_r, hid_s, hid_r, tk_s, tk_r,
    tg_s, tg_r, sum_s, sum_r, one_s, one_r, two_s, two_r,
):
    d, r, c = lax.axis_index("dp"), lax.axis_index("row"), lax.axis_index("col")
    group = n_dp * n_row
    k = d * n_row + r
    tokens, columns = cot.shape
    shard = tokens // n_col
    own = tokens // group
    units = hid.shape[1]
    ranks = basis.shape[0]
    own_ranks = ranks // group
    row_ranks = ranks // n_col
    tiles = units // tile
    hops = n_col // 2

    def around(me, offset, n):
        return lax.rem(me + offset + n, n)

    odd = lax.rem(c, 2)
    pos = (1 - odd) * lax.div(c, 2) + odd * (n_col - 1 - lax.div(c, 2))

    def at_pos(q):
        upper = lax.div(q, hops)
        return (1 - upper) * (2 * q) + upper * (2 * (n_col - 1 - q) + 1)

    def ring_col(offset):
        return at_pos(around(pos, offset, n_col))

    barrier = pltpu.get_barrier_semaphore()
    for o in range(1, n_col):
        pl.semaphore_signal(barrier, inc=1, device_id=(d, r, around(c, o, n_col)), device_id_type=pl.DeviceIdType.MESH)
    for o in range(1, n_row):
        pl.semaphore_signal(barrier, inc=1, device_id=(d, around(r, o, n_row), c), device_id_type=pl.DeviceIdType.MESH)
    for o in range(1, n_dp):
        pl.semaphore_signal(barrier, inc=1, device_id=(around(d, o, n_dp), r, c), device_id_type=pl.DeviceIdType.MESH)
    pl.semaphore_wait(barrier, n_col + n_row + n_dp - 3)

    sent = []

    def start(copy):
        copy.start()
        sent.append(copy)

    def rows_of(col_index):
        return cot.at[pl.ds(pl.multiple_of(col_index * shard, shard), shard)]

    def half_of(col_index, which):
        return cot.at[pl.ds(pl.multiple_of(col_index * shard + which * (shard // 2), shard // 2), shard // 2)]

    def ring_copy(step, way):
        sign = 1 - 2 * way
        source = ring_col(-sign * (step - 1))
        target = (d, r, ring_col(sign))
        if step == hops:
            dst = half_of(source, way)
            src = dst if step > 1 else cot_in.at[pl.ds(way * (shard // 2), shard // 2)]
        else:
            dst = rows_of(source)
            src = dst if step > 1 else cot_in
        return remote(src, dst, ring_s.at[way, step - 1], ring_r.at[way, step - 1], target)

    def ring_arrived(step, way):
        sign = 1 - 2 * way
        source = ring_col(-sign * step)
        ref = half_of(source, way) if step == hops else rows_of(source)
        remote(ref, ref, ring_s.at[way, step - 1], ring_r.at[way, step - 1], (d, r, ring_col(sign))).wait_recv()

    def gather_start(src, slot, send, recv):
        for o in range(1, n_dp):
            start(remote(src, slot(k), send.at[o - 1], recv.at[k], (around(d, o, n_dp), r, c)))
        for o in range(1, n_row):
            start(remote(src, slot(k), send.at[n_dp - 1 + o - 1], recv.at[k], (d, around(r, o, n_row), c)))

    def gather_pass(slot, send, recv):
        for j in range(1, n_dp):
            block = around(d, -j, n_dp) * n_row + r
            remote(slot(block), slot(block), send.at[0], recv.at[block], (around(d, j, n_dp), r, c)).wait_recv()
            for o in range(1, n_row):
                start(remote(
                    slot(block), slot(block), send.at[n_dp - 1 + j * (n_row - 1) + o - 1], recv.at[block],
                    (d, around(r, o, n_row), c),
                ))

    def gather_end(slot, send, recv):
        for j in range(n_dp):
            for o in range(1, n_row):
                block = around(d, -j, n_dp) * n_row + around(r, -o, n_row)
                remote(slot(block), slot(block), send.at[0], recv.at[block], (d, around(r, o, n_row), c)).wait_recv()

    def basis_slot(block):
        return basis.at[pl.ds(pl.multiple_of(block * own_ranks, own_ranks), own_ranks)]

    def hid_slot(block):
        return hid.at[pl.ds(pl.multiple_of(block * own, own), own)]

    def tok_slot(block):
        return tok_all.at[block]

    start(ring_copy(1, 0))
    start(ring_copy(1, 1))
    gather_start(basis_in, basis_slot, bas_s, bas_r)
    own_cot = pltpu.make_async_copy(cot_in, rows_of(c), local_sem.at[0])
    own_cot.start()
    own_basis = pltpu.make_async_copy(basis_in, basis_slot(k), local_sem.at[1])
    own_basis.start()

    def weight_copy(t):
        return pltpu.make_async_copy(
            weight.at[pl.ds(pl.multiple_of(t * tile, tile), tile)], wt.at[t], w_sem.at[t])

    for t in range(tiles):
        weight_copy(t).start()

    @pl.loop(0, tiles)
    def _(t):
        at = pl.ds(pl.multiple_of(t * tile, tile), tile)
        gate_f = gate[:, at].astype(jnp.float32)
        act = gate_f * jax.nn.sigmoid(gate_f)
        hid[pl.ds(pl.multiple_of(k * own, own), own), at] = (act * up[:, at].astype(jnp.float32)).astype(jnp.bfloat16)

    step = 1

    def ring_step():
        nonlocal step
        if step > hops:
            return
        for way in (0, 1):
            ring_arrived(step, way)
            if step < hops:
                start(ring_copy(step + 1, way))
        step += 1

    ring_step()
    gather_pass(basis_slot, bas_s, bas_r)
    gather_start(hid_slot(k), hid_slot, hid_s, hid_r)
    own_basis.wait()
    gather_end(basis_slot, bas_s, bas_r)

    token_part = lax.dot_general(
        basis[...], hid[pl.ds(pl.multiple_of(k * own, own), own)], CONTRACT_LAST,
        preferred_element_type=jnp.float32)
    for j in range(n_col):
        tok_send[j] = token_part[j * row_ranks:(j + 1) * row_ranks].astype(jnp.bfloat16)
    for o in range(1, n_col):
        peer = around(c, o, n_col)
        start(remote(tok_send.at[peer], tok_recv.at[c], tk_s.at[o - 1], tk_r.at[c], (d, r, peer)))
    ring_step()
    total = tok_send[c].astype(jnp.float32)
    for o in range(1, n_col):
        peer = around(c, -o, n_col)
        remote(tok_recv.at[peer], tok_recv.at[peer], tk_s.at[o - 1], tk_r.at[peer], (d, r, around(c, o, n_col))).wait_recv()
        total = total + tok_recv[peer].astype(jnp.float32)
    tok_all[k] = total.astype(jnp.bfloat16)
    gather_start(tok_slot(k), tok_slot, tg_s, tg_r)
    ring_step()
    gather_pass(tok_slot, tg_s, tg_r)
    gather_end(tok_slot, tg_s, tg_r)
    while step <= hops:
        ring_step()
    own_cot.wait()
    cot_write = pltpu.make_async_copy(cot, cot_out, local_sem.at[2])
    cot_write.start()
    gather_pass(hid_slot, hid_s, hid_r)

    token_all = jnp.concatenate([tok_all[j] for j in range(group)], axis=1)

    @pl.loop(0, columns // wide)
    def _(j):
        at = pl.ds(pl.multiple_of(j * wide, wide), wide)
        projected = jnp.dot(token_all, cot[:, at], preferred_element_type=jnp.float32)
        first = 0.9 * first_in[:, at] + 0.1 * projected
        second = 0.999 * second_in[:, at] + 0.001 * projected * projected
        adapted = first / first_fix / (jnp.sqrt(second / second_fix) + 1e-06)
        first_out[:, at] = first
        second_out[:, at] = second
        sums[c, 0:1, at] = jnp.sum(adapted * adapted, axis=0, keepdims=True)
        sums[c, 1:2, at] = jnp.sum(projected * projected, axis=0, keepdims=True)

    for o in range(1, n_col):
        start(remote(sums.at[c], sums.at[c], sum_s.at[o - 1], sum_r.at[c], (d, r, around(c, o, n_col))))

    def one_copy(t, o):
        peer = around(r, o, n_row)
        return remote(part.at[t, peer], recv1.at[t, r], one_s.at[t, o - 1], one_r.at[t, r], (d, peer, c))

    def two_copy(t, o):
        peer = around(d, o, n_dp)
        return remote(half.at[t, peer], recv2.at[t, d], two_s.at[t, o - 1], two_r.at[t, d], (peer, r, c))

    def product(t):
        weight_copy(t).wait()
        out = lax.dot_general(cot[...], wt[t], CONTRACT_LAST, preferred_element_type=jnp.float32)
        for e in range(n_dp):
            for f in range(n_row):
                begin = (e * n_row + f) * own
                part[t, f, e] = out[begin:begin + own].astype(jnp.bfloat16)
        for o in range(1, n_row):
            one_copy(t, o).start()

    def sum_row(t):
        for o in range(1, n_row):
            peer = around(r, -o, n_row)
            ref = recv1.at[t, peer]
            remote(ref, ref, one_s.at[t, o - 1], one_r.at[t, peer], (d, around(r, o, n_row), c)).wait_recv()
        for e in range(n_dp):
            total = part[t, r, e].astype(jnp.float32)
            for o in range(1, n_row):
                total = total + recv1[t, around(r, -o, n_row), e].astype(jnp.float32)
            half[t, e] = total.astype(jnp.bfloat16)
        for o in range(1, n_dp):
            two_copy(t, o).start()

    def sum_dp(t):
        total = half[t, d].astype(jnp.float32)
        for o in range(1, n_dp):
            peer = around(d, -o, n_dp)
            ref = recv2.at[t, peer]
            remote(ref, ref, two_s.at[t, o - 1], two_r.at[t, peer], (around(d, o, n_dp), r, c)).wait_recv()
            total = total + recv2[t, peer].astype(jnp.float32)
        grad_hidden = total.astype(jnp.bfloat16).astype(jnp.float32)
        at = pl.ds(pl.multiple_of(t * tile, tile), tile)
        gate_f = gate[:, at].astype(jnp.float32)
        up_f = up[:, at].astype(jnp.float32)
        sigma = jax.nn.sigmoid(gate_f)
        grad_up[:, at] = (grad_hidden * (gate_f * sigma)).astype(jnp.bfloat16)
        grad_gate[:, at] = (grad_hidden * up_f * sigma * (1.0 + gate_f * (1.0 - sigma))).astype(jnp.bfloat16)

    @pl.loop(0, tiles)
    def _(t):
        product(t)

        @pl.when(t >= 1)
        def _():
            sum_row(t - 1)

        @pl.when(t >= 2)
        def _():
            sum_dp(t - 2)

    sum_row(tiles - 1)
    gather_end(hid_slot, hid_s, hid_r)
    hid_write = pltpu.make_async_copy(hid, hid_out, local_sem.at[3])
    hid_write.start()
    for o in range(1, n_col):
        peer = around(c, -o, n_col)
        remote(sums.at[peer], sums.at[peer], sum_s.at[o - 1], sum_r.at[peer], (d, r, around(c, o, n_col))).wait_recv()
    total = sums[0]
    for j in range(1, n_col):
        total = total + sums[j]
    scale_out[...] = jnp.sqrt(total[0:1]) / (jnp.sqrt(total[1:2]) + 1e-06)

    @pl.loop(max(tiles - 2, 0), tiles)
    def _(t):
        sum_dp(t)

    for copy in sent:
        copy.wait_send()

    @pl.loop(0, tiles)
    def _(t):
        for o in range(1, n_row):
            one_copy(t, o).wait_send()
        for o in range(1, n_dp):
            two_copy(t, o).wait_send()

    cot_write.wait()
    hid_write.wait()


def shards(n_dp, n_row, n_col, gate_pre, up_pre, grad_out, down_weight, basis, first_moment_in, second_moment_in):
    own, units = gate_pre.shape
    shard, columns = grad_out.shape
    row_ranks = first_moment_in.shape[0]
    ranks = row_ranks * n_col
    tokens = shard * n_col
    group = n_dp * n_row
    tile = width_of(units, 512)
    wide = width_of(columns, 512)
    tiles = units // tile
    sends = max(1, n_dp - 1 + n_dp * (n_row - 1))
    hops = n_col // 2
    bf16, f32 = jnp.bfloat16, jnp.float32
    vmem = pl.BlockSpec(memory_space=pltpu.VMEM)
    hbm = pl.BlockSpec(memory_space=pl.ANY)
    dma = pltpu.SemaphoreType.DMA
    grad_gate, grad_up, first_moment, second_moment, scale, cot, hid = pl.pallas_call(
        functools.partial(kernel, n_dp, n_row, n_col, tile, wide),
        out_shape=(
            jax.ShapeDtypeStruct((own, units), bf16),
            jax.ShapeDtypeStruct((own, units), bf16),
            jax.ShapeDtypeStruct((row_ranks, columns), f32),
            jax.ShapeDtypeStruct((row_ranks, columns), f32),
            jax.ShapeDtypeStruct((1, columns), f32),
            jax.ShapeDtypeStruct((tokens, columns), bf16),
            jax.ShapeDtypeStruct((tokens, units), bf16),
        ),
        in_specs=[vmem, vmem, hbm, hbm, hbm, vmem, vmem],
        out_specs=[vmem, vmem, vmem, vmem, vmem, hbm, hbm],
        scratch_shapes=[
            pltpu.VMEM((tokens, columns), bf16),
            pltpu.VMEM((tokens, units), bf16),
            pltpu.VMEM((ranks, units), bf16),
            pltpu.VMEM((tiles, tile, columns), bf16),
            pltpu.VMEM((tiles, n_row, n_dp, own, tile), bf16),
            pltpu.VMEM((tiles, n_row, n_dp, own, tile), bf16),
            pltpu.VMEM((tiles, n_dp, own, tile), bf16),
            pltpu.VMEM((tiles, n_dp, own, tile), bf16),
            pltpu.VMEM((n_col, row_ranks, own), bf16),
            pltpu.VMEM((n_col, row_ranks, own), bf16),
            pltpu.VMEM((group, row_ranks, own), bf16),
            pltpu.VMEM((n_col, 2, columns), f32),
            dma((4,)),
            dma((tiles,)),
            dma((2, hops)),
            dma((2, hops)),
            dma((sends,)),
            dma((group,)),
            dma((sends,)),
            dma((group,)),
            dma((n_col,)),
            dma((n_col,)),
            dma((sends,)),
            dma((group,)),
            dma((n_col,)),
            dma((n_col,)),
            dma((tiles, n_row)),
            dma((tiles, n_row)),
            dma((tiles, n_dp)),
            dma((tiles, n_dp)),
        ],
        compiler_params=pltpu.CompilerParams(
            collective_id=0, has_side_effects=True, vmem_limit_bytes=63 * 1024 * 1024
        ),
        cost_estimate=pl.CostEstimate(
            flops=2 * tokens * columns * units, bytes_accessed=2 * columns * units, transcendentals=0
        ),
    )(gate_pre, up_pre, grad_out, down_weight, basis, first_moment_in, second_moment_in)
    grad_weight = lax.dot_general(
        hid, cot, (((0,), (0,)), ((), ())), preferred_element_type=jnp.float32
    ).astype(jnp.bfloat16)
    scaled_grad = (grad_weight.astype(jnp.float32) * scale).astype(jnp.bfloat16)
    return (grad_gate, grad_up, scaled_grad, first_moment, second_moment)


def solution(mesh):
    split, by_col = P(("dp", "row"), "col"), P("col", ("dp", "row"))
    return jax.shard_map(
        functools.partial(shards, mesh.shape["dp"], mesh.shape["row"], mesh.shape["col"]),
        mesh=mesh,
        in_specs=(split, split, by_col, by_col, split, by_col, by_col),
        out_specs=(split, split, by_col, by_col, by_col),
        check_vma=False,
    )
```

```python
import functools
import math

import jax
import jax.numpy as jnp
from jax import lax
from jax.experimental import pallas as pl
from jax.experimental.pallas import tpu as pltpu
from jax.sharding import PartitionSpec as P

first_fix = 1.0 - math.exp(1000.0 * math.log(0.9))
second_fix = 1.0 - math.exp(1000.0 * math.log(0.999))

CONTRACT_LAST = (((1,), (1,)), ((), ()))


def width_of(extent, most):
    best = 128
    for width in range(128, most + 1, 128):
        if extent % width == 0:
            best = width
    return best


def remote(src, dst, send_sem, recv_sem, device):
    return pltpu.make_async_remote_copy(
        src_ref=src,
        dst_ref=dst,
        send_sem=send_sem,
        recv_sem=recv_sem,
        device_id=device,
        device_id_type=pl.DeviceIdType.MESH,
    )


def kernel(
    n_dp, n_row, n_col, tile, wide,
    gate, up, cot_in, weight, basis_in, first_in, second_in,
    grad_gate, grad_up, first_out, second_out, scale_out, cot_out, hid_out,
    cot, hid, basis, wt, part, recv1, half, recv2, tok_send, tok_recv, tok_all, sums,
    local_sem, w_sem, ring_s, ring_r, bas_s, bas_r, hid_s, hid_r, tk_s, tk_r,
    tg_s, tg_r, sum_s, sum_r, one_s, one_r, two_s, two_r,
):
    d, r, c = lax.axis_index("dp"), lax.axis_index("row"), lax.axis_index("col")
    group = n_dp * n_row
    k = d * n_row + r
    tokens, columns = cot.shape
    shard = tokens // n_col
    own = tokens // group
    units = hid.shape[1]
    ranks = basis.shape[0]
    own_ranks = ranks // group
    row_ranks = ranks // n_col
    tiles = units // tile
    hops = n_col // 2

    def around(me, offset, n):
        return lax.rem(me + offset + n, n)

    odd = lax.rem(c, 2)
    pos = (1 - odd) * lax.div(c, 2) + odd * (n_col - 1 - lax.div(c, 2))

    def at_pos(q):
        upper = lax.div(q, hops)
        return (1 - upper) * (2 * q) + upper * (2 * (n_col - 1 - q) + 1)

    def ring_col(offset):
        return at_pos(around(pos, offset, n_col))

    barrier = pltpu.get_barrier_semaphore()
    for o in range(1, n_col):
        pl.semaphore_signal(barrier, inc=1, device_id=(d, r, around(c, o, n_col)), device_id_type=pl.DeviceIdType.MESH)
    for o in range(1, n_row):
        pl.semaphore_signal(barrier, inc=1, device_id=(d, around(r, o, n_row), c), device_id_type=pl.DeviceIdType.MESH)
    for o in range(1, n_dp):
        pl.semaphore_signal(barrier, inc=1, device_id=(around(d, o, n_dp), r, c), device_id_type=pl.DeviceIdType.MESH)
    pl.semaphore_wait(barrier, n_col + n_row + n_dp - 3)

    sent = []

    def start(copy):
        copy.start()
        sent.append(copy)

    def rows_of(col_index):
        return cot.at[pl.ds(pl.multiple_of(col_index * shard, shard), shard)]

    def half_of(col_index, which):
        return cot.at[pl.ds(pl.multiple_of(col_index * shard + which * (shard // 2), shard // 2), shard // 2)]

    def ring_copy(step, way):
        sign = 1 - 2 * way
        source = ring_col(-sign * (step - 1))
        target = (d, r, ring_col(sign))
        if step == hops:
            dst = half_of(source, way)
            src = dst if step > 1 else cot_in.at[pl.ds(way * (shard // 2), shard // 2)]
        else:
            dst = rows_of(source)
            src = dst if step > 1 else cot_in
        return remote(src, dst, ring_s.at[way, step - 1], ring_r.at[way, step - 1], target)

    def ring_arrived(step, way):
        sign = 1 - 2 * way
        source = ring_col(-sign * step)
        ref = half_of(source, way) if step == hops else rows_of(source)
        remote(ref, ref, ring_s.at[way, step - 1], ring_r.at[way, step - 1], (d, r, ring_col(sign))).wait_recv()

    def gather_start(src, slot, send, recv):
        for o in range(1, n_dp):
            start(remote(src, slot(k), send.at[o - 1], recv.at[k], (around(d, o, n_dp), r, c)))
        for o in range(1, n_row):
            start(remote(src, slot(k), send.at[n_dp - 1 + o - 1], recv.at[k], (d, around(r, o, n_row), c)))

    def gather_pass(slot, send, recv):
        for j in range(1, n_dp):
            block = around(d, -j, n_dp) * n_row + r
            remote(slot(block), slot(block), send.at[0], recv.at[block], (around(d, j, n_dp), r, c)).wait_recv()
            for o in range(1, n_row):
                start(remote(
                    slot(block), slot(block), send.at[n_dp - 1 + j * (n_row - 1) + o - 1], recv.at[block],
                    (d, around(r, o, n_row), c),
                ))

    def gather_end(slot, send, recv):
        for j in range(n_dp):
            for o in range(1, n_row):
                block = around(d, -j, n_dp) * n_row + around(r, -o, n_row)
                remote(slot(block), slot(block), send.at[0], recv.at[block], (d, around(r, o, n_row), c)).wait_recv()

    def basis_slot(block):
        return basis.at[pl.ds(pl.multiple_of(block * own_ranks, own_ranks), own_ranks)]

    def hid_slot(block):
        return hid.at[pl.ds(pl.multiple_of(block * own, own), own)]

    def tok_slot(block):
        return tok_all.at[block]

    start(ring_copy(1, 0))
    start(ring_copy(1, 1))
    gather_start(basis_in, basis_slot, bas_s, bas_r)
    own_cot = pltpu.make_async_copy(cot_in, rows_of(c), local_sem.at[0])
    own_cot.start()
    own_basis = pltpu.make_async_copy(basis_in, basis_slot(k), local_sem.at[1])
    own_basis.start()

    def weight_copy(t):
        return pltpu.make_async_copy(
            weight.at[pl.ds(pl.multiple_of(t * tile, tile), tile)], wt.at[t], w_sem.at[t])

    for t in range(tiles):
        weight_copy(t).start()

    @pl.loop(0, tiles)
    def _(t):
        at = pl.ds(pl.multiple_of(t * tile, tile), tile)
        gate_f = gate[:, at].astype(jnp.float32)
        act = gate_f * jax.nn.sigmoid(gate_f)
        hid[pl.ds(pl.multiple_of(k * own, own), own), at] = (act * up[:, at].astype(jnp.float32)).astype(jnp.bfloat16)

    step = 1

    def ring_step():
        nonlocal step
        if step > hops:
            return
        for way in (0, 1):
            ring_arrived(step, way)
            if step < hops:
                start(ring_copy(step + 1, way))
        step += 1

    ring_step()
    gather_pass(basis_slot, bas_s, bas_r)
    gather_start(hid_slot(k), hid_slot, hid_s, hid_r)
    own_basis.wait()
    gather_end(basis_slot, bas_s, bas_r)

    token_part = lax.dot_general(
        basis[...], hid[pl.ds(pl.multiple_of(k * own, own), own)], CONTRACT_LAST,
        preferred_element_type=jnp.float32)
    for j in range(n_col):
        tok_send[j] = token_part[j * row_ranks:(j + 1) * row_ranks].astype(jnp.bfloat16)
    for o in range(1, n_col):
        peer = around(c, o, n_col)
        start(remote(tok_send.at[peer], tok_recv.at[c], tk_s.at[o - 1], tk_r.at[c], (d, r, peer)))
    def token_sum():
        total = tok_send[c].astype(jnp.float32)
        for o in range(1, n_col):
            peer = around(c, -o, n_col)
            remote(tok_recv.at[peer], tok_recv.at[peer], tk_s.at[o - 1], tk_r.at[peer], (d, r, around(c, o, n_col))).wait_recv()
            total = total + tok_recv[peer].astype(jnp.float32)
        tok_all[k] = total.astype(jnp.bfloat16)
        gather_start(tok_slot(k), tok_slot, tg_s, tg_r)

    def project():
        token_all = jnp.concatenate([tok_all[j] for j in range(group)], axis=1)

        @pl.loop(0, columns // wide)
        def _(j):
            at = pl.ds(pl.multiple_of(j * wide, wide), wide)
            projected = jnp.dot(token_all, cot[:, at], preferred_element_type=jnp.float32)
            first = 0.9 * first_in[:, at] + 0.1 * projected
            second = 0.999 * second_in[:, at] + 0.001 * projected * projected
            adapted = first / first_fix / (jnp.sqrt(second / second_fix) + 1e-06)
            first_out[:, at] = first
            second_out[:, at] = second
            sums[c, 0:1, at] = jnp.sum(adapted * adapted, axis=0, keepdims=True)
            sums[c, 1:2, at] = jnp.sum(projected * projected, axis=0, keepdims=True)

        for o in range(1, n_col):
            start(remote(sums.at[c], sums.at[c], sum_s.at[o - 1], sum_r.at[c], (d, r, around(c, o, n_col))))

    per = own // shard
    early_steps = hops // 2
    order = [0]
    for o in range(1, hops):
        order += [-o, o]
    order += [hops]
    early = 2 * early_steps + 1
    groups = (range(0, early), range(early, n_col))

    def place(i):
        q = ring_col(order[i])
        block = lax.div(q, per)
        return q, lax.div(block, n_row), lax.rem(block, n_row), lax.rem(q, per)

    def one_copy(t, i):
        q, e, f, sub = place(i)
        slot = e * per + sub
        return remote(part.at[t, i], recv1.at[t, r, slot], one_s.at[t, i], one_r.at[t, r, slot], (d, f, c))

    def two_copy(t, i):
        q, e, f, sub = place(i)
        slot = e * per + sub
        return remote(half.at[t, slot], recv2.at[t, d, sub], two_s.at[t, slot], two_r.at[t, d, sub], (e, r, c))

    def product(g, t):
        if g == 0:
            weight_copy(t).wait()
        slots = groups[g]
        left = jnp.concatenate(
            [rows_of(ring_col(order[i]))[...] for i in slots], axis=0)
        out = lax.dot_general(left, wt[t], CONTRACT_LAST, preferred_element_type=jnp.float32)
        for n, i in enumerate(slots):
            part[t, i] = out[n * shard:(n + 1) * shard].astype(jnp.bfloat16)
        for i in slots:
            f = place(i)[2]

            @pl.when(f != r)
            def _():
                one_copy(t, i).start()

    def sum_row(g, t):
        for i in groups[g]:
            q, e, f, sub = place(i)
            slot = e * per + sub

            @pl.when(f == r)
            def _():
                total = part[t, i].astype(jnp.float32)
                for o in range(1, n_row):
                    peer = around(r, -o, n_row)
                    ref = recv1.at[t, peer, slot]
                    remote(ref, ref, one_s.at[t, i], one_r.at[t, peer, slot], (d, around(r, o, n_row), c)).wait_recv()
                    total = total + recv1[t, peer, slot].astype(jnp.float32)
                half[t, slot] = total.astype(jnp.bfloat16)

                @pl.when(e != d)
                def _():
                    two_copy(t, i).start()

    def sum_dp(g, t):
        for i in groups[g]:
            q, e, f, sub = place(i)

            @pl.when(e * n_row + f == k)
            def _():
                total = half[t, e * per + sub].astype(jnp.float32)
                for o in range(1, n_dp):
                    peer = around(d, -o, n_dp)
                    ref = recv2.at[t, peer, sub]
                    remote(ref, ref, two_s.at[t, 0], two_r.at[t, peer, sub], (around(d, o, n_dp), r, c)).wait_recv()
                    total = total + recv2[t, peer, sub].astype(jnp.float32)
                grad_hidden = total.astype(jnp.bfloat16).astype(jnp.float32)
                at = pl.ds(pl.multiple_of(t * tile, tile), tile)
                rows = pl.ds(pl.multiple_of(sub * shard, shard), shard)
                gate_f = gate[rows, at].astype(jnp.float32)
                up_f = up[rows, at].astype(jnp.float32)
                sigma = jax.nn.sigmoid(gate_f)
                grad_up[rows, at] = (grad_hidden * (gate_f * sigma)).astype(jnp.bfloat16)
                grad_gate[rows, at] = (
                    grad_hidden * up_f * sigma * (1.0 + gate_f * (1.0 - sigma))).astype(jnp.bfloat16)

    def early_tiles(begin, end):
        @pl.loop(begin, end)
        def _(t):
            product(0, t)

            @pl.when(t >= 1)
            def _():
                sum_row(0, t - 1)

    def late_tiles(begin, end):
        @pl.loop(begin, end)
        def _(t):
            product(1, t)

            @pl.when(t >= 1)
            def _():
                sum_row(1, t - 1)

            sum_dp(0, t)

    own_cot.wait()
    while step <= early_steps:
        ring_step()
    cut = min(4, tiles)
    early_tiles(0, cut)
    ring_step()
    token_sum()
    early_tiles(cut, tiles)
    while step <= hops:
        ring_step()
    cot_write = pltpu.make_async_copy(cot, cot_out, local_sem.at[2])
    cot_write.start()
    gather_pass(tok_slot, tg_s, tg_r)
    gather_pass(hid_slot, hid_s, hid_r)
    sum_row(0, tiles - 1)
    gather_end(tok_slot, tg_s, tg_r)
    late_tiles(0, cut)
    project()
    late_tiles(cut, tiles)
    sum_row(1, tiles - 1)
    gather_end(hid_slot, hid_s, hid_r)
    hid_write = pltpu.make_async_copy(hid, hid_out, local_sem.at[3])
    hid_write.start()
    for o in range(1, n_col):
        peer = around(c, -o, n_col)
        remote(sums.at[peer], sums.at[peer], sum_s.at[o - 1], sum_r.at[peer], (d, r, around(c, o, n_col))).wait_recv()
    total = sums[0]
    for j in range(1, n_col):
        total = total + sums[j]
    scale_out[...] = jnp.sqrt(total[0:1]) / (jnp.sqrt(total[1:2]) + 1e-06)

    @pl.loop(0, tiles)
    def _(t):
        sum_dp(1, t)

    for copy in sent:
        copy.wait_send()

    @pl.loop(0, tiles)
    def _(t):
        for i in range(n_col):
            q, e, f, sub = place(i)

            @pl.when(f != r)
            def _():
                one_copy(t, i).wait_send()

            @pl.when((f == r) & (e != d))
            def _():
                two_copy(t, i).wait_send()

    cot_write.wait()
    hid_write.wait()


def shards(n_dp, n_row, n_col, gate_pre, up_pre, grad_out, down_weight, basis, first_moment_in, second_moment_in):
    own, units = gate_pre.shape
    shard, columns = grad_out.shape
    row_ranks = first_moment_in.shape[0]
    ranks = row_ranks * n_col
    tokens = shard * n_col
    group = n_dp * n_row
    tile = width_of(units, 512)
    wide = width_of(columns, 512)
    tiles = units // tile
    sends = max(1, n_dp - 1 + n_dp * (n_row - 1))
    hops = n_col // 2
    per = own // shard
    bf16, f32 = jnp.bfloat16, jnp.float32
    vmem = pl.BlockSpec(memory_space=pltpu.VMEM)
    hbm = pl.BlockSpec(memory_space=pl.ANY)
    dma = pltpu.SemaphoreType.DMA
    grad_gate, grad_up, first_moment, second_moment, scale, cot, hid = pl.pallas_call(
        functools.partial(kernel, n_dp, n_row, n_col, tile, wide),
        out_shape=(
            jax.ShapeDtypeStruct((own, units), bf16),
            jax.ShapeDtypeStruct((own, units), bf16),
            jax.ShapeDtypeStruct((row_ranks, columns), f32),
            jax.ShapeDtypeStruct((row_ranks, columns), f32),
            jax.ShapeDtypeStruct((1, columns), f32),
            jax.ShapeDtypeStruct((tokens, columns), bf16),
            jax.ShapeDtypeStruct((tokens, units), bf16),
        ),
        in_specs=[vmem, vmem, hbm, hbm, hbm, vmem, vmem],
        out_specs=[vmem, vmem, vmem, vmem, vmem, hbm, hbm],
        scratch_shapes=[
            pltpu.VMEM((tokens, columns), bf16),
            pltpu.VMEM((tokens, units), bf16),
            pltpu.VMEM((ranks, units), bf16),
            pltpu.VMEM((tiles, tile, columns), bf16),
            pltpu.VMEM((tiles, n_col, shard, tile), bf16),
            pltpu.VMEM((tiles, n_row, n_dp * per, shard, tile), bf16),
            pltpu.VMEM((tiles, n_dp * per, shard, tile), bf16),
            pltpu.VMEM((tiles, n_dp, per, shard, tile), bf16),
            pltpu.VMEM((n_col, row_ranks, own), bf16),
            pltpu.VMEM((n_col, row_ranks, own), bf16),
            pltpu.VMEM((group, row_ranks, own), bf16),
            pltpu.VMEM((n_col, 2, columns), f32),
            dma((4,)),
            dma((tiles,)),
            dma((2, hops)),
            dma((2, hops)),
            dma((sends,)),
            dma((group,)),
            dma((sends,)),
            dma((group,)),
            dma((n_col,)),
            dma((n_col,)),
            dma((sends,)),
            dma((group,)),
            dma((n_col,)),
            dma((n_col,)),
            dma((tiles, n_col)),
            dma((tiles, n_row, n_dp * per)),
            dma((tiles, n_dp * per)),
            dma((tiles, n_dp, per)),
        ],
        compiler_params=pltpu.CompilerParams(
            collective_id=0, has_side_effects=True, vmem_limit_bytes=63 * 1024 * 1024
        ),
        cost_estimate=pl.CostEstimate(
            flops=2 * tokens * columns * units, bytes_accessed=2 * columns * units, transcendentals=0
        ),
    )(gate_pre, up_pre, grad_out, down_weight, basis, first_moment_in, second_moment_in)
    grad_weight = lax.dot_general(
        hid, cot, (((0,), (0,)), ((), ())), preferred_element_type=jnp.float32
    ).astype(jnp.bfloat16)
    scaled_grad = (grad_weight.astype(jnp.float32) * scale).astype(jnp.bfloat16)
    return (grad_gate, grad_up, scaled_grad, first_moment, second_moment)


def solution(mesh):
    split, by_col = P(("dp", "row"), "col"), P("col", ("dp", "row"))
    return jax.shard_map(
        functools.partial(shards, mesh.shape["dp"], mesh.shape["row"], mesh.shape["col"]),
        mesh=mesh,
        in_specs=(split, split, by_col, by_col, split, by_col, by_col),
        out_specs=(split, split, by_col, by_col, by_col),
        check_vma=False,
    )
```

```python
import functools
import math

import jax
import jax.numpy as jnp
from jax import lax
from jax.experimental import pallas as pl
from jax.experimental.pallas import tpu as pltpu
from jax.sharding import PartitionSpec as P

first_fix = 1.0 - math.exp(1000.0 * math.log(0.9))
second_fix = 1.0 - math.exp(1000.0 * math.log(0.999))

CONTRACT_LAST = (((1,), (1,)), ((), ()))


def width_of(extent, most):
    best = 128
    for width in range(128, most + 1, 128):
        if extent % width == 0:
            best = width
    return best


def remote(src, dst, send_sem, recv_sem, device):
    return pltpu.make_async_remote_copy(
        src_ref=src,
        dst_ref=dst,
        send_sem=send_sem,
        recv_sem=recv_sem,
        device_id=device,
        device_id_type=pl.DeviceIdType.MESH,
    )


def kernel(
    n_dp, n_row, n_col, tile, wide,
    gate, up, cot_in, weight, basis_in, first_in, second_in,
    grad_gate, grad_up, first_out, second_out, scale_out, cot_out, hid_out,
    cot, hid, basis, wt, part, recv1, half, recv2, tok_send, tok_recv, tok_all, sums,
    local_sem, w_sem, ring_s, ring_r, bas_s, bas_r, hid_s, hid_r, tk_s, tk_r,
    tg_s, tg_r, sum_s, sum_r, one_s, one_r, two_s, two_r,
):
    d, r, c = lax.axis_index("dp"), lax.axis_index("row"), lax.axis_index("col")
    group = n_dp * n_row
    k = d * n_row + r
    tokens, columns = cot.shape
    shard = tokens // n_col
    own = tokens // group
    units = hid.shape[1]
    ranks = basis.shape[0]
    own_ranks = ranks // group
    row_ranks = ranks // n_col
    tiles = units // tile
    hops = n_col // 2
    early_steps = hops // 2

    def around(me, offset, n):
        return lax.rem(me + offset + n, n)

    odd = lax.rem(c, 2)
    pos = (1 - odd) * lax.div(c, 2) + odd * (n_col - 1 - lax.div(c, 2))

    def at_pos(q):
        upper = lax.div(q, hops)
        return (1 - upper) * (2 * q) + upper * (2 * (n_col - 1 - q) + 1)

    def ring_col(offset):
        return at_pos(around(pos, offset, n_col))

    barrier = pltpu.get_barrier_semaphore()
    for o in range(1, n_col):
        pl.semaphore_signal(barrier, inc=1, device_id=(d, r, around(c, o, n_col)), device_id_type=pl.DeviceIdType.MESH)
    for o in range(1, n_row):
        pl.semaphore_signal(barrier, inc=1, device_id=(d, around(r, o, n_row), c), device_id_type=pl.DeviceIdType.MESH)
    for o in range(1, n_dp):
        pl.semaphore_signal(barrier, inc=1, device_id=(around(d, o, n_dp), r, c), device_id_type=pl.DeviceIdType.MESH)
    pl.semaphore_wait(barrier, n_col + n_row + n_dp - 3)

    sent = []

    def start(copy):
        copy.start()
        sent.append(copy)

    def rows_of(col_index):
        return cot.at[pl.ds(pl.multiple_of(col_index * shard, shard), shard)]

    def half_of(col_index, which):
        return cot.at[pl.ds(pl.multiple_of(col_index * shard + which * (shard // 2), shard // 2), shard // 2)]

    def ring_copy(step, way):
        sign = 1 - 2 * way
        source = ring_col(-sign * (step - 1))
        target = (d, r, ring_col(sign))
        if step == hops:
            dst = half_of(source, way)
            src = dst if step > 1 else cot_in.at[pl.ds(way * (shard // 2), shard // 2)]
        else:
            dst = rows_of(source)
            src = dst if step > 1 else cot_in
        return remote(src, dst, ring_s.at[way, step - 1], ring_r.at[way, step - 1], target)

    def ring_arrived(step, way):
        sign = 1 - 2 * way
        source = ring_col(-sign * step)
        ref = half_of(source, way) if step == hops else rows_of(source)
        remote(ref, ref, ring_s.at[way, step - 1], ring_r.at[way, step - 1], (d, r, ring_col(sign))).wait_recv()

    def gather_start(src, slot, send, recv):
        for o in range(1, n_dp):
            start(remote(src, slot(k), send.at[o - 1], recv.at[k], (around(d, o, n_dp), r, c)))
        for o in range(1, n_row):
            start(remote(src, slot(k), send.at[n_dp - 1 + o - 1], recv.at[k], (d, around(r, o, n_row), c)))

    def gather_pass(slot, send, recv):
        for j in range(1, n_dp):
            block = around(d, -j, n_dp) * n_row + r
            remote(slot(block), slot(block), send.at[0], recv.at[block], (around(d, j, n_dp), r, c)).wait_recv()
            for o in range(1, n_row):
                start(remote(
                    slot(block), slot(block), send.at[n_dp - 1 + j * (n_row - 1) + o - 1], recv.at[block],
                    (d, around(r, o, n_row), c),
                ))

    def gather_end(slot, send, recv):
        for j in range(n_dp):
            for o in range(1, n_row):
                block = around(d, -j, n_dp) * n_row + around(r, -o, n_row)
                remote(slot(block), slot(block), send.at[0], recv.at[block], (d, around(r, o, n_row), c)).wait_recv()

    def basis_slot(block):
        return basis.at[pl.ds(pl.multiple_of(block * own_ranks, own_ranks), own_ranks)]

    def hid_slot(block):
        return hid.at[pl.ds(pl.multiple_of(block * own, own), own)]

    def tok_slot(block):
        return tok_all.at[block]

    start(ring_copy(1, 0))
    start(ring_copy(1, 1))
    gather_start(basis_in, basis_slot, bas_s, bas_r)
    own_cot = pltpu.make_async_copy(cot_in, rows_of(c), local_sem.at[0])
    own_cot.start()
    own_basis = pltpu.make_async_copy(basis_in, basis_slot(k), local_sem.at[1])
    own_basis.start()

    def weight_copy(t):
        return pltpu.make_async_copy(
            weight.at[pl.ds(pl.multiple_of(t * tile, tile), tile)], wt.at[t], w_sem.at[t])

    for t in range(tiles):
        weight_copy(t).start()

    @pl.loop(0, tiles)
    def _(t):
        at = pl.ds(pl.multiple_of(t * tile, tile), tile)
        gate_f = gate[:, at].astype(jnp.float32)
        act = gate_f * jax.nn.sigmoid(gate_f)
        hid[pl.ds(pl.multiple_of(k * own, own), own), at] = (act * up[:, at].astype(jnp.float32)).astype(jnp.bfloat16)

    step = 1

    def ring_step():
        nonlocal step
        if step > hops:
            return
        for way in (0, 1):
            ring_arrived(step, way)
            if step < hops:
                start(ring_copy(step + 1, way))
        step += 1

    ring_step()
    gather_pass(basis_slot, bas_s, bas_r)
    gather_start(hid_slot(k), hid_slot, hid_s, hid_r)
    if early_steps > 1:
        ring_step()
    own_basis.wait()
    gather_end(basis_slot, bas_s, bas_r)

    token_part = lax.dot_general(
        basis[...], hid[pl.ds(pl.multiple_of(k * own, own), own)], CONTRACT_LAST,
        preferred_element_type=jnp.float32)
    for j in range(n_col):
        tok_send[j] = token_part[j * row_ranks:(j + 1) * row_ranks].astype(jnp.bfloat16)
    for o in range(1, n_col):
        peer = around(c, o, n_col)
        start(remote(tok_send.at[peer], tok_recv.at[c], tk_s.at[o - 1], tk_r.at[c], (d, r, peer)))
    def token_sum():
        total = tok_send[c].astype(jnp.float32)
        for o in range(1, n_col):
            peer = around(c, -o, n_col)
            remote(tok_recv.at[peer], tok_recv.at[peer], tk_s.at[o - 1], tk_r.at[peer], (d, r, around(c, o, n_col))).wait_recv()
            total = total + tok_recv[peer].astype(jnp.float32)
        tok_all[k] = total.astype(jnp.bfloat16)
        gather_start(tok_slot(k), tok_slot, tg_s, tg_r)

    def project():
        token_all = jnp.concatenate([tok_all[j] for j in range(group)], axis=1)

        @pl.loop(0, columns // wide)
        def _(j):
            at = pl.ds(pl.multiple_of(j * wide, wide), wide)
            projected = jnp.dot(token_all, cot[:, at], preferred_element_type=jnp.float32)
            first = 0.9 * first_in[:, at] + 0.1 * projected
            second = 0.999 * second_in[:, at] + 0.001 * projected * projected
            adapted = first / first_fix / (jnp.sqrt(second / second_fix) + 1e-06)
            first_out[:, at] = first
            second_out[:, at] = second
            sums[c, 0:1, at] = jnp.sum(adapted * adapted, axis=0, keepdims=True)
            sums[c, 1:2, at] = jnp.sum(projected * projected, axis=0, keepdims=True)

        for o in range(1, n_col):
            start(remote(sums.at[c], sums.at[c], sum_s.at[o - 1], sum_r.at[c], (d, r, around(c, o, n_col))))

    per = own // shard
    order = [0]
    for o in range(1, hops):
        order += [-o, o]
    order += [hops]
    early = 2 * early_steps + 1
    groups = (range(0, early), range(early, n_col))

    def place(i):
        q = ring_col(order[i])
        block = lax.div(q, per)
        return q, lax.div(block, n_row), lax.rem(block, n_row), lax.rem(q, per)

    def one_copy(t, i):
        q, e, f, sub = place(i)
        slot = e * per + sub
        return remote(part.at[t, i], recv1.at[t, r, slot], one_s.at[t, i], one_r.at[t, r, slot], (d, f, c))

    def two_copy(t, i):
        q, e, f, sub = place(i)
        slot = e * per + sub
        return remote(half.at[t, slot], recv2.at[t, d, sub], two_s.at[t, slot], two_r.at[t, d, sub], (e, r, c))

    def product(g, t):
        if g == 0:
            weight_copy(t).wait()
        slots = groups[g]
        left = jnp.concatenate(
            [rows_of(ring_col(order[i]))[...] for i in slots], axis=0)
        out = lax.dot_general(left, wt[t], CONTRACT_LAST, preferred_element_type=jnp.float32)
        for n, i in enumerate(slots):
            part[t, i] = out[n * shard:(n + 1) * shard].astype(jnp.bfloat16)
        for i in slots:
            f = place(i)[2]

            @pl.when(f != r)
            def _():
                one_copy(t, i).start()

    def sum_row(g, t):
        for i in groups[g]:
            q, e, f, sub = place(i)
            slot = e * per + sub

            @pl.when(f == r)
            def _():
                total = part[t, i].astype(jnp.float32)
                for o in range(1, n_row):
                    peer = around(r, -o, n_row)
                    ref = recv1.at[t, peer, slot]
                    remote(ref, ref, one_s.at[t, i], one_r.at[t, peer, slot], (d, around(r, o, n_row), c)).wait_recv()
                    total = total + recv1[t, peer, slot].astype(jnp.float32)
                half[t, slot] = total.astype(jnp.bfloat16)

                @pl.when(e != d)
                def _():
                    two_copy(t, i).start()

    def sum_dp(g, t):
        for i in groups[g]:
            q, e, f, sub = place(i)

            @pl.when(e * n_row + f == k)
            def _():
                total = half[t, e * per + sub].astype(jnp.float32)
                for o in range(1, n_dp):
                    peer = around(d, -o, n_dp)
                    ref = recv2.at[t, peer, sub]
                    remote(ref, ref, two_s.at[t, 0], two_r.at[t, peer, sub], (around(d, o, n_dp), r, c)).wait_recv()
                    total = total + recv2[t, peer, sub].astype(jnp.float32)
                grad_hidden = total.astype(jnp.bfloat16).astype(jnp.float32)
                at = pl.ds(pl.multiple_of(t * tile, tile), tile)
                rows = pl.ds(pl.multiple_of(sub * shard, shard), shard)
                gate_f = gate[rows, at].astype(jnp.float32)
                up_f = up[rows, at].astype(jnp.float32)
                sigma = jax.nn.sigmoid(gate_f)
                grad_up[rows, at] = (grad_hidden * (gate_f * sigma)).astype(jnp.bfloat16)
                grad_gate[rows, at] = (
                    grad_hidden * up_f * sigma * (1.0 + gate_f * (1.0 - sigma))).astype(jnp.bfloat16)

    def early_tiles(begin, end):
        @pl.loop(begin, end)
        def _(t):
            product(0, t)

            @pl.when(t >= 1)
            def _():
                sum_row(0, t - 1)

    def late_tiles(begin, end):
        @pl.loop(begin, end)
        def _(t):
            product(1, t)

            @pl.when(t >= 1)
            def _():
                sum_row(1, t - 1)

            sum_dp(0, t)

    own_cot.wait()
    while step <= early_steps:
        ring_step()
    cut = min(3, tiles)
    early_tiles(0, cut)
    ring_step()
    token_sum()
    early_tiles(cut, tiles)
    while step <= hops:
        ring_step()
    cot_write = pltpu.make_async_copy(cot, cot_out, local_sem.at[2])
    cot_write.start()
    gather_pass(tok_slot, tg_s, tg_r)
    gather_pass(hid_slot, hid_s, hid_r)
    sum_row(0, tiles - 1)
    gather_end(tok_slot, tg_s, tg_r)
    late_tiles(0, cut)
    project()
    late_tiles(cut, tiles)
    sum_row(1, tiles - 1)
    gather_end(hid_slot, hid_s, hid_r)
    hid_write = pltpu.make_async_copy(hid, hid_out, local_sem.at[3])
    hid_write.start()
    for o in range(1, n_col):
        peer = around(c, -o, n_col)
        remote(sums.at[peer], sums.at[peer], sum_s.at[o - 1], sum_r.at[peer], (d, r, around(c, o, n_col))).wait_recv()
    total = sums[0]
    for j in range(1, n_col):
        total = total + sums[j]
    scale_out[...] = jnp.sqrt(total[0:1]) / (jnp.sqrt(total[1:2]) + 1e-06)

    @pl.loop(0, tiles)
    def _(t):
        sum_dp(1, t)

    for copy in sent:
        copy.wait_send()

    @pl.loop(0, tiles)
    def _(t):
        for i in range(n_col):
            q, e, f, sub = place(i)

            @pl.when(f != r)
            def _():
                one_copy(t, i).wait_send()

            @pl.when((f == r) & (e != d))
            def _():
                two_copy(t, i).wait_send()

    cot_write.wait()
    hid_write.wait()


def shards(n_dp, n_row, n_col, gate_pre, up_pre, grad_out, down_weight, basis, first_moment_in, second_moment_in):
    own, units = gate_pre.shape
    shard, columns = grad_out.shape
    row_ranks = first_moment_in.shape[0]
    ranks = row_ranks * n_col
    tokens = shard * n_col
    group = n_dp * n_row
    tile = width_of(units, 512)
    wide = width_of(columns, 512)
    tiles = units // tile
    sends = max(1, n_dp - 1 + n_dp * (n_row - 1))
    hops = n_col // 2
    per = own // shard
    bf16, f32 = jnp.bfloat16, jnp.float32
    vmem = pl.BlockSpec(memory_space=pltpu.VMEM)
    hbm = pl.BlockSpec(memory_space=pl.ANY)
    dma = pltpu.SemaphoreType.DMA
    grad_gate, grad_up, first_moment, second_moment, scale, cot, hid = pl.pallas_call(
        functools.partial(kernel, n_dp, n_row, n_col, tile, wide),
        out_shape=(
            jax.ShapeDtypeStruct((own, units), bf16),
            jax.ShapeDtypeStruct((own, units), bf16),
            jax.ShapeDtypeStruct((row_ranks, columns), f32),
            jax.ShapeDtypeStruct((row_ranks, columns), f32),
            jax.ShapeDtypeStruct((1, columns), f32),
            jax.ShapeDtypeStruct((tokens, columns), bf16),
            jax.ShapeDtypeStruct((tokens, units), bf16),
        ),
        in_specs=[vmem, vmem, hbm, hbm, hbm, vmem, vmem],
        out_specs=[vmem, vmem, vmem, vmem, vmem, hbm, hbm],
        scratch_shapes=[
            pltpu.VMEM((tokens, columns), bf16),
            pltpu.VMEM((tokens, units), bf16),
            pltpu.VMEM((ranks, units), bf16),
            pltpu.VMEM((tiles, tile, columns), bf16),
            pltpu.VMEM((tiles, n_col, shard, tile), bf16),
            pltpu.VMEM((tiles, n_row, n_dp * per, shard, tile), bf16),
            pltpu.VMEM((tiles, n_dp * per, shard, tile), bf16),
            pltpu.VMEM((tiles, n_dp, per, shard, tile), bf16),
            pltpu.VMEM((n_col, row_ranks, own), bf16),
            pltpu.VMEM((n_col, row_ranks, own), bf16),
            pltpu.VMEM((group, row_ranks, own), bf16),
            pltpu.VMEM((n_col, 2, columns), f32),
            dma((4,)),
            dma((tiles,)),
            dma((2, hops)),
            dma((2, hops)),
            dma((sends,)),
            dma((group,)),
            dma((sends,)),
            dma((group,)),
            dma((n_col,)),
            dma((n_col,)),
            dma((sends,)),
            dma((group,)),
            dma((n_col,)),
            dma((n_col,)),
            dma((tiles, n_col)),
            dma((tiles, n_row, n_dp * per)),
            dma((tiles, n_dp * per)),
            dma((tiles, n_dp, per)),
        ],
        compiler_params=pltpu.CompilerParams(
            collective_id=0, has_side_effects=True, vmem_limit_bytes=63 * 1024 * 1024
        ),
        cost_estimate=pl.CostEstimate(
            flops=2 * tokens * columns * units, bytes_accessed=2 * columns * units, transcendentals=0
        ),
    )(gate_pre, up_pre, grad_out, down_weight, basis, first_moment_in, second_moment_in)
    grad_weight = lax.dot_general(
        hid, cot, (((0,), (0,)), ((), ())), preferred_element_type=jnp.float32
    ).astype(jnp.bfloat16)
    scaled_grad = (grad_weight.astype(jnp.float32) * scale).astype(jnp.bfloat16)
    return (grad_gate, grad_up, scaled_grad, first_moment, second_moment)


def solution(mesh):
    split, by_col = P(("dp", "row"), "col"), P("col", ("dp", "row"))
    return jax.shard_map(
        functools.partial(shards, mesh.shape["dp"], mesh.shape["row"], mesh.shape["col"]),
        mesh=mesh,
        in_specs=(split, split, by_col, by_col, split, by_col, by_col),
        out_specs=(split, split, by_col, by_col, by_col),
        check_vma=False,
    )
```
